512 devices in a mesh: clus: 128 (over y, z, core), rep: 4 (over x).
Axes of the slice: x: 4, y: 8, z: 8, core: 2. Of those that a mesh axis runs over, the one named last changes fastest.
Arguments:
- start_vector: bfloat16 [131072, 128], P('clus'), may hold values from -6 to 6
- self_term: float32 [131072], P('clus'), may hold values from 0.5 to 1.5
- near_blocks: bfloat16 [4096, 256, 256], P(('clus', 'rep')), may hold values from -0.09375 to 0.09375
- near_pairs: int32 [4096, 2], P(('clus', 'rep')), may hold values from 0 to 7, as said below
- far_factor: bfloat16 [128, 4, 128, 32, 256], P('clus', 'rep'), may hold values from -0.1875 to 0.1875
- far_cluster: int32 [128, 4, 128], P('clus', 'rep'), may hold values from 0 to 3
Outputs:
- first_image: bfloat16 [131072, 128], P('clus')
- second_image: bfloat16 [131072, 128], P('clus')
The draws below stay inside these ranges and needn't reach their ends.
Inputs may be any that keep to these rules, and one draw needn't show every extreme that they name: `near_pairs`: column 0 lies in 0 to 3; column 1 is at least column 0 and below 8, and below 4 for pairs of the last slab.
All inputs are finite; a program needn't handle non-finite values.
Results may differ from the reference program's by a relative error of at most 0.01.
Values may be sent and summed in bfloat16 or wider, within the bound.
A program may use at most 64 MiB of HBM per device.

```python
import math
import jax
import jax.numpy as jnp
from jax import lax

CLUSTER = 256
RANK = 32
RHS = 128
CL_DEV = 4
NP_DEV = 8
FAR_DEV = 128
SLOTS = 1
NCLUSTERS = 512
PANELS = 131072
NEAR = 4096
N_CLUS = 128
N_REP = 4


def draw_near_pairs(key, part):
    key = jax.random.fold_in(key, 11)
    first_key, second_key = jax.random.split(key)
    total = N_CLUS * N_REP * NP_DEV
    owner = jnp.arange(total, dtype=jnp.int32) // (N_REP * NP_DEV)
    span = jnp.where(owner == N_CLUS - 1, CL_DEV, 2 * CL_DEV).astype(jnp.int32)
    row_part = jax.random.randint(first_key, (total,), 0, CL_DEV, dtype=jnp.int32)
    offset = jax.random.randint(second_key, (total,), 0, 1048576, dtype=jnp.int32) % (span - row_part)
    return jnp.stack([row_part, row_part + offset], axis=1).astype(jnp.int32)


def with_ends(entries, rng, smallest, high):
    spot = [jax.random.randint(jax.random.fold_in(rng, axis), (), 0, length) for axis, length in enumerate(entries.shape)]
    longest = entries.shape.index(max(entries.shape))
    beside = spot[:longest] + [(spot[longest] + 1) % entries.shape[longest]] + spot[longest + 1:]
    return entries.at[tuple(spot)].set(smallest).at[tuple(beside)].set(high)


def shard_levels(own_key, dims, pieces, least, top_value):
    loudness = 1.0
    for position, shards_of in pieces:
        steps = jax.random.uniform(jax.random.fold_in(jax.random.fold_in(own_key, 6), position), (shards_of,), jnp.float32, least / len(pieces), top_value / len(pieces))
        loudness = loudness * jnp.repeat(jnp.exp(steps), dims[position] // shards_of).reshape((-1,) + (1,) * (len(dims) - 1 - position))
    return loudness


def normal_values(key, dims, scale, reach, shards=(), kind=jnp.bfloat16):
    loudness = shard_levels(key, dims, shards, -0.22, 0.18) if shards else 1.0
    values = jax.random.normal(key, dims, jnp.float32) * scale * loudness
    return jnp.minimum(jnp.maximum(values, -reach), reach).astype(kind)


def setup_inputs(seed: int = 0) -> dict:
    keys = jax.random.split(jax.random.key(seed), 7)
    start_vector = normal_values(keys[0], (PANELS, RHS), 1.0, 6.0, ((0, 128),))
    self_term = jnp.clip(jnp.exp(math.log(1.5) - 1.0986123 * jax.random.uniform(keys[1], (PANELS,), jnp.float32) ** shard_levels(keys[1], (PANELS,), ((0, 128),), -0.2, 0.2)), 0.5, 1.5)
    near_blocks = normal_values(keys[2], (NEAR, CLUSTER, CLUSTER), (CLUSTER * 16) ** -0.5, 0.09375, ((0, 512),))
    near_pairs = draw_near_pairs(jax.random.fold_in(keys[6], 71), 0)
    far_factor = normal_values(keys[4], (N_CLUS, N_REP, FAR_DEV, RANK, CLUSTER), (CLUSTER * 4) ** -0.5, 0.1875, ((0, 128), (1, 4)))
    far_cluster = with_ends(jax.random.randint(keys[5], (N_CLUS, N_REP, FAR_DEV), 0, CL_DEV), jax.random.fold_in(keys[5], 1), 0, CL_DEV - 1).astype(jnp.int32)
    return dict(start_vector=start_vector, self_term=self_term, near_blocks=near_blocks, near_pairs=near_pairs, far_factor=far_factor, far_cluster=far_cluster)


def apply_operator(vector, self_term, near_blocks, near_pairs, far_factor, far_cluster):
    slabs = vector.reshape(NCLUSTERS, CLUSTER, RHS)
    groups = N_CLUS * N_REP
    blocks = near_blocks.reshape(groups, NP_DEV, CLUSTER, CLUSTER)
    pairs = near_pairs.reshape(groups, NP_DEV, 2).astype(jnp.int32)

    def near_step(total, item):
        group, block, pair = item
        base = (group // N_REP) * CL_DEV
        left = (base + pair[:, 0]).astype(jnp.int32)
        right = (base + pair[:, 1]).astype(jnp.int32)
        matrix = block.astype(jnp.float32)
        forward = jnp.einsum("pab,pbr->par", matrix, slabs[right].astype(jnp.float32))
        backward = jnp.einsum("pba,pbr->par", matrix, slabs[left].astype(jnp.float32))
        total = total.at[left].add(forward)
        total = total.at[right].add(backward)
        return total, None

    start_total = jnp.zeros((NCLUSTERS, CLUSTER, RHS), jnp.float32)
    near_total, _ = lax.scan(near_step, start_total, (jnp.arange(groups, dtype=jnp.int32), blocks, pairs))

    slab_view = slabs.reshape(N_CLUS, CL_DEV, CLUSTER, RHS)

    def coef_one(item):
        factors, owners, values = item
        picked = values[owners.astype(jnp.int32)].astype(jnp.float32)
        return jnp.einsum("sqkn,sqnr->sqkr", factors.astype(jnp.float32), picked).astype(jnp.bfloat16)

    coef = lax.map(coef_one, (far_factor, far_cluster, slab_view))
    partner = coef.reshape(N_CLUS, N_REP, N_CLUS, SLOTS, RANK, RHS).transpose(2, 1, 0, 3, 4, 5)
    partner = partner.reshape(N_CLUS, N_REP, FAR_DEV, RANK, RHS)

    def apply_one(item):
        factors, owners, received = item
        spread = jnp.einsum("sqkn,sqkr->sqnr", factors.astype(jnp.float32), received.astype(jnp.float32))
        table = (owners[:, :, None] == jnp.arange(CL_DEV, dtype=jnp.int32)[None, None, :]).astype(jnp.float32)
        return jnp.einsum("sqc,sqnr->cnr", table, spread)

    far_total = lax.map(apply_one, (far_factor, far_cluster, partner)).reshape(NCLUSTERS, CLUSTER, RHS)
    own = self_term.reshape(NCLUSTERS, CLUSTER, 1) * slabs.astype(jnp.float32)
    result = own + near_total + far_total
    return result.astype(jnp.bfloat16).reshape(PANELS, RHS)


def reference(start_vector, self_term, near_blocks, near_pairs, far_factor, far_cluster):
    first_image = apply_operator(start_vector, self_term, near_blocks, near_pairs, far_factor, far_cluster)
    second_image = apply_operator(first_image, self_term, near_blocks, near_pairs, far_factor, far_cluster)
    return (first_image, second_image)
```

```python
import functools

import jax
import jax.numpy as jnp
from jax import lax
from jax.experimental import pallas as pl
from jax.experimental.pallas import tpu as pltpu
from jax.sharding import PartitionSpec as P

MESH = pl.DeviceIdType.MESH
BF16 = jnp.bfloat16
F32 = jnp.float32

SLABS = 128
REPS = 4
SIDE = 8
CLUSTERS = 4
SIZE = 256
COLS = 128
GROUPS = 2
HALF = COLS // GROUPS
WIDE = CLUSTERS * HALF
QUARTER = SIZE // REPS
RANK = 32
PAIRS = 8
CHUNK = 8


def wrap(value):
    value = jnp.where(value >= SIDE, value - SIDE, value)
    return jnp.where(value < 0, value + SIDE, value)


def to_all_slabs(slab, send):
    core = lax.rem(slab, 2)
    z = lax.rem(slab // 2, SIDE)
    y = slab // (2 * SIDE)

    def to(a, b, other):
        send((wrap(y + a) * SIDE + wrap(z + b)) * 2 + other)

    def four(i, _):
        j = 15 - i // 2
        other = lax.rem(core + i, 2)
        a = 1 + j // 4
        b = lax.rem(j, 4)
        to(a, b, other)
        to(-a, -b, other)
        to(-b, a, other)
        to(b, -a, other)
        return 0

    lax.fori_loop(0, 6, four, 0)
    for other in (0, 1):
        to(4, 0, other)
        to(0, 4, other)
        to(4, 4, other)
    lax.fori_loop(8, 32, four, 0)
    send(slab + 1 - 2 * core)


def swap_halves(x):
    return pltpu.roll(x, HALF, 1)


def kernel(
    pairs, owners, start_in, self_in, near_in, far_in, first_out, second_out,
    start, self_row, near, near_t, far, far_t, vec, self_wide, masks,
    sbuf, rbuf, nextvec, doubled, spread, fwd, bwd, acc, nx_part, nx_got, ns_out, ns_got, xr, result,
    load_sem, out_sem, a2a_s, a2a_r, x_s, x_r, vn_s, vn_r, rl_s, rl_r, nx_s, nx_r, ns_s, ns_r,
):
    slab, rep = lax.axis_index("clus"), lax.axis_index("rep")
    after = jnp.where(slab == SLABS - 1, 0, slab + 1)
    before = jnp.where(slab == 0, SLABS - 1, slab - 1)
    rep_peers = [lax.rem(rep + k, REPS) for k in (2, 1, 3)]

    loads = [
        pltpu.make_async_copy(start_in, start, load_sem.at[0]),
        pltpu.make_async_copy(far_in, far, load_sem.at[1]),
        pltpu.make_async_copy(self_in, self_row, load_sem.at[2]),
    ] + [
        pltpu.make_async_copy(near_in.at[n], near.at[:, pl.ds(n * SIZE, SIZE)], load_sem.at[3 + n])
        for n in range(PAIRS)
    ]
    for load in loads:
        load.start()

    greeting = pltpu.get_barrier_semaphore()

    def greet(peer):
        pl.semaphore_signal(greeting, inc=1, device_id=(peer, rep), device_id_type=MESH)

    to_all_slabs(slab, greet)
    for peer in rep_peers:
        pl.semaphore_signal(greeting, inc=1, device_id=(slab, peer), device_id_type=MESH)

    lane = lax.broadcasted_iota(jnp.int32, (16, COLS), 1)
    low = (lane < HALF).astype(F32).astype(BF16)
    high = (lane >= HALF).astype(F32).astype(BF16)
    block = lax.broadcasted_iota(jnp.int32, (16, 2 * WIDE), 1) // HALF
    for c in range(2 * CLUSTERS):
        masks[c] = (block == c).astype(F32).astype(BF16)

    def merged(x, y):
        rows = x.shape[0]
        x3, y3 = x.reshape(rows // 16, 16, COLS), y.reshape(rows // 16, 16, COLS)
        return (x3 * low[None] + y3 * high[None]).reshape(rows, COLS)

    loads[0].wait()
    for pair in range(CLUSTERS // 2):
        even = start[pl.ds(2 * pair * SIZE, SIZE), :]
        odd = start[pl.ds((2 * pair + 1) * SIZE, SIZE), :]
        part = (REPS, QUARTER, COLS)
        vec[0, 0, :, :, pl.ds(pair * COLS, COLS)] = merged(even, swap_halves(odd)).reshape(part)
        vec[0, 1, :, :, pl.ds(pair * COLS, COLS)] = merged(swap_halves(even), odd).reshape(part)

    def coefficients(m, g):
        values = vec[m, g].reshape(SIZE, WIDE)

        def step(t, _):
            factors = far[pl.ds(t * CHUNK, CHUNK)].reshape(CHUNK * RANK, SIZE)
            full = jnp.dot(factors, values, preferred_element_type=F32).astype(BF16)
            for e in range(CHUNK):
                end = t * CHUNK + e
                mask = masks[owners[end], :, pl.ds(0, WIDE)]
                halves = []
                for top in (0, 16):
                    rows = full[e * RANK + top : e * RANK + top + 16, :] * mask
                    folded = rows[:, :COLS] + rows[:, COLS:]
                    halves.append(folded + swap_halves(folded))
                sbuf[m, g, end] = halves[0] * low + halves[1] * high
            return 0

        lax.fori_loop(0, SLABS // CHUNK, step, 0)
        rbuf[m, g, slab] = sbuf[m, g, slab]

    def send_coefficients(m, g):
        def send(peer):
            pltpu.make_async_remote_copy(
                sbuf.at[m, g, peer], rbuf.at[m, g, slab], a2a_s.at[m, g], a2a_r.at[m, g],
                device_id=(peer, rep), device_id_type=MESH,
            ).start()

        to_all_slabs(slab, send)

    def all_coefficients(m, g):
        others = pl.ds(0, SLABS - 1)
        return pltpu.make_async_remote_copy(
            sbuf.at[m, g, others], rbuf.at[m, g, others], a2a_s.at[m, g], a2a_r.at[m, g],
            device_id=(slab, rep), device_id_type=MESH,
        )

    def next_vector(m, g):
        return pltpu.make_async_remote_copy(
            vec.at[m, g, rep], nextvec.at[m, g, rep], vn_s.at[m, g], vn_r.at[m, g],
            device_id=(before, rep), device_id_type=MESH,
        )

    def relays(m, g):
        return [
            pltpu.make_async_remote_copy(
                nextvec.at[m, g, rep], nextvec.at[m, g, rep], rl_s.at[m, g, k], rl_r.at[m, g, k],
                device_id=(slab, peer), device_id_type=MESH,
            )
            for k, peer in enumerate(rep_peers)
        ]

    def next_parts(m, g):
        return [
            pltpu.make_async_remote_copy(
                nx_part.at[m, g, peer], nx_got.at[m, g, rep], nx_s.at[m, g, k], nx_r.at[m, g, k],
                device_id=(slab, peer), device_id_type=MESH,
            )
            for k, peer in enumerate(rep_peers)
        ]

    def next_sum(m, g):
        return pltpu.make_async_remote_copy(
            ns_out.at[m, g], ns_got.at[m, g], ns_s.at[m, g], ns_r.at[m, g],
            device_id=(after, rep), device_id_type=MESH,
        )

    def exchanges(m, g):
        return [
            pltpu.make_async_remote_copy(
                xr.at[m, g, rep], xr.at[m, g, rep], x_s.at[m, g, k], x_r.at[m, g, k],
                device_id=(slab, peer), device_id_type=MESH,
            )
            for k, peer in enumerate(rep_peers)
        ]

    def near_terms(m, g):
        for base, source in ((0, vec), (CLUSTERS, nextvec)):
            for pair in range(CLUSTERS // 2):
                both = source[m, g, :, :, pl.ds(pair * COLS, COLS)].reshape(SIZE, COLS)
                turned = swap_halves(both)
                doubled[base + 2 * pair] = merged(both, turned)
                doubled[base + 2 * pair + 1] = merged(turned, both)

        def place(n, _):
            a, b = pairs[n, 0], pairs[n, 1]
            tall = (SIZE // 16, 16, COLS)
            column, row = doubled[b].reshape(tall), doubled[a].reshape(tall)
            for k in range(WIDE // COLS):
                mask = masks[a, :, pl.ds(k * COLS, COLS)]
                fwd[n, :, pl.ds(k * COLS, COLS)] = (column * mask[None]).reshape(SIZE, COLS)
            for k in range(2 * WIDE // COLS):
                mask = masks[b, :, pl.ds(k * COLS, COLS)]
                bwd[n, :, pl.ds(k * COLS, COLS)] = (row * mask[None]).reshape(SIZE, COLS)
            return 0

        lax.fori_loop(0, PAIRS, place, 0)
        deep = PAIRS * SIZE
        backward = jnp.dot(near_t[...], bwd[...].reshape(deep, 2 * WIDE), preferred_element_type=F32)
        nx_part[m, g] = backward[:, WIDE:].astype(BF16).reshape(REPS, QUARTER, WIDE)
        acc[m, g] = backward[:, :WIDE]
        acc[m, g] += jnp.dot(near[...], fwd[...].reshape(deep, WIDE), preferred_element_type=F32)
        nx_got[m, g, rep] = nx_part[m, g, rep]
        for copy in next_parts(m, g):
            copy.start()

    def sum_next(m, g):
        for copy in next_parts(m, g):
            copy.wait_recv()
        total = nx_got[m, g, 0].astype(F32)
        for s in range(1, REPS):
            total += nx_got[m, g, s].astype(F32)
        ns_out[m, g] = total.astype(BF16)
        next_sum(m, g).start()

    def far_terms(m, g):
        all_coefficients(m, g).wait_recv()

        def step(t, _):
            for e in range(CHUNK):
                end = t * CHUNK + e
                mask = masks[owners[end], :, pl.ds(0, WIDE)]
                got = rbuf[m, g, end]
                turned = swap_halves(got)
                upper = got * low + turned * high
                lower = turned * low + got * high
                for k in range(WIDE // COLS):
                    part = mask[:, k * COLS : (k + 1) * COLS]
                    lanes = pl.ds(k * COLS, COLS)
                    spread[t, pl.ds(e * RANK, 16), lanes] = upper * part
                    spread[t, pl.ds(e * RANK + 16, 16), lanes] = lower * part
            return 0

        lax.fori_loop(0, SLABS // CHUNK, step, 0)
        total = acc[m, g]
        for q in range(4):
            total += jnp.dot(
                far_t[q], spread[pl.ds(4 * q, 4)].reshape(4 * CHUNK * RANK, WIDE), preferred_element_type=F32
            )
        acc[m, g] = total
        next_sum(m, g).wait_recv()
        mine = pl.ds(pl.multiple_of(rep * QUARTER, QUARTER), QUARTER)
        acc[m, g, mine, :] += ns_got[m, g].astype(F32)
        xr[m, g, rep] = acc[m, g].astype(BF16)
        for copy in exchanges(m, g):
            copy.start()

    def image(m, g):
        for copy in exchanges(m, g):
            copy.wait_recv()
        total = self_wide[...] * vec[m, g].reshape(SIZE, WIDE).astype(F32)
        for s in range(REPS):
            total += xr[m, g, s].astype(F32)
        vec[m + 1, g] = total.astype(BF16).reshape(REPS, QUARTER, WIDE)

    def write(m, out):
        for pair in range(CLUSTERS // 2):
            lanes = pl.ds(pair * COLS, COLS)
            a = vec[m + 1, 0, :, :, lanes].reshape(SIZE, COLS)
            b = vec[m + 1, 1, :, :, lanes].reshape(SIZE, COLS)
            result[m, pl.ds(2 * pair * SIZE, SIZE), :] = merged(a, swap_halves(b))
            result[m, pl.ds((2 * pair + 1) * SIZE, SIZE), :] = merged(swap_halves(a), b)
        pltpu.make_async_copy(result.at[m], out, out_sem.at[m]).start()

    loads[1].wait()
    coefficients(0, 0)
    pl.semaphore_wait(greeting, SLABS - 1 + REPS - 1)
    next_vector(0, 0).start()
    next_vector(0, 1).start()
    send_coefficients(0, 0)
    coefficients(0, 1)
    send_coefficients(0, 1)

    for load in loads[2:]:
        load.wait()
    for n in range(PAIRS):
        near_t[:, pl.ds(n * SIZE, SIZE)] = near[:, pl.ds(n * SIZE, SIZE)].T
    for t in range(SLABS // CHUNK):
        tile = far[pl.ds(t * CHUNK, CHUNK)].reshape(CHUNK * RANK, SIZE)
        far_t[t // 4, :, pl.ds((t % 4) * CHUNK * RANK, CHUNK * RANK)] = tile.T
    wide = [
        jnp.broadcast_to(
            jnp.concatenate([self_row[2 * c : 2 * c + 1, :], self_row[2 * c + 1 : 2 * c + 2, :]], axis=1),
            (HALF, SIZE),
        )
        for c in range(CLUSTERS)
    ]
    self_wide[...] = jnp.concatenate(wide, axis=0).T

    def pass_on(m, g):
        next_vector(m, g).wait_recv()
        for copy in relays(m, g):
            copy.start()

    def near_part(m, g):
        for copy in relays(m, g):
            copy.wait_recv()
        near_terms(m, g)

    pass_on(0, 0)
    pass_on(0, 1)
    near_part(0, 0)
    near_part(0, 1)
    sum_next(0, 0)
    sum_next(0, 1)
    far_terms(0, 0)
    image(0, 0)
    next_vector(1, 0).start()
    coefficients(1, 0)
    send_coefficients(1, 0)
    far_terms(0, 1)
    pass_on(1, 0)
    image(0, 1)
    next_vector(1, 1).start()
    coefficients(1, 1)
    send_coefficients(1, 1)
    write(0, first_out)
    pass_on(1, 1)
    near_part(1, 0)
    near_part(1, 1)
    sum_next(1, 0)
    sum_next(1, 1)
    far_terms(1, 0)
    image(1, 0)
    far_terms(1, 1)
    image(1, 1)
    write(1, second_out)

    for m in range(2):
        for g in range(GROUPS):
            all_coefficients(m, g).wait_send()
            next_vector(m, g).wait_send()
            next_sum(m, g).wait_send()
            for copy in relays(m, g) + next_parts(m, g) + exchanges(m, g):
                copy.wait_send()
    pltpu.make_async_copy(result.at[0], first_out, out_sem.at[0]).wait()
    pltpu.make_async_copy(result.at[1], second_out, out_sem.at[1]).wait()


def local(start_vector, self_term, near_blocks, near_pairs, far_factor, far_cluster):
    panels, columns = start_vector.shape
    factors = far_factor.reshape(far_factor.shape[2:])
    owners = far_cluster.reshape(-1)
    self_rows = self_term.reshape(panels // COLS, COLS)
    vmem, dma = pltpu.VMEM, pltpu.SemaphoreType.DMA
    image = jax.ShapeDtypeStruct((panels, columns), BF16)
    both = (2, GROUPS)
    scratch = [
        vmem((panels, columns), BF16),
        vmem(self_rows.shape, F32),
        vmem((SIZE, PAIRS * SIZE), BF16),
        vmem((SIZE, PAIRS * SIZE), BF16),
        vmem(factors.shape, BF16),
        vmem((4, SIZE, SLABS // 4 * RANK), BF16),
        vmem((3, GROUPS, REPS, QUARTER, WIDE), BF16),
        vmem((SIZE, WIDE), F32),
        vmem((2 * CLUSTERS, 16, 2 * WIDE), BF16),
        vmem(both + (SLABS, 16, COLS), BF16),
        vmem(both + (SLABS, 16, COLS), BF16),
        vmem(both + (REPS, QUARTER, WIDE), BF16),
        vmem((2 * CLUSTERS, SIZE, COLS), BF16),
        vmem((SLABS // CHUNK, CHUNK * RANK, WIDE), BF16),
        vmem((PAIRS, SIZE, WIDE), BF16),
        vmem((PAIRS, SIZE, 2 * WIDE), BF16),
        vmem(both + (SIZE, WIDE), F32),
        vmem(both + (REPS, QUARTER, WIDE), BF16),
        vmem(both + (REPS, QUARTER, WIDE), BF16),
        vmem(both + (QUARTER, WIDE), BF16),
        vmem(both + (QUARTER, WIDE), BF16),
        vmem(both + (REPS, SIZE, WIDE), BF16),
        vmem((2, panels, columns), BF16),
        dma((3 + PAIRS,)),
        dma((2,)),
        dma(both), dma(both),
        dma(both + (3,)), dma(both + (3,)),
        dma(both), dma(both),
        dma(both + (3,)), dma(both + (3,)),
        dma(both + (3,)), dma(both + (3,)),
        dma(both), dma(both),
    ]
    smem = pl.BlockSpec(memory_space=pltpu.SMEM)
    hbm = pl.BlockSpec(memory_space=pl.ANY)
    return pl.pallas_call(
        kernel,
        out_shape=(image, image),
        in_specs=[smem, smem, hbm, hbm, hbm, hbm],
        out_specs=(hbm, hbm),
        scratch_shapes=scratch,
        compiler_params=pltpu.CompilerParams(
            collective_id=0, has_side_effects=True, vmem_limit_bytes=52 * 1024 * 1024
        ),
        name="two_products",
    )(near_pairs, owners, start_vector, self_rows, near_blocks, factors)


def solution(mesh):
    placed = (
        P("clus", None),
        P("clus"),
        P(("clus", "rep"), None, None),
        P(("clus", "rep"), None),
        P("clus", "rep", None, None, None),
        P("clus", "rep", None),
    )
    return jax.shard_map(
        local,
        mesh=mesh,
        in_specs=placed,
        out_specs=(P("clus", None), P("clus", None)),
        check_vma=False,
    )
```

```python
import functools

import jax
import jax.numpy as jnp
from jax import lax
from jax.experimental import pallas as pl
from jax.experimental.pallas import tpu as pltpu
from jax.sharding import PartitionSpec as P

MESH = pl.DeviceIdType.MESH
BF16 = jnp.bfloat16
F32 = jnp.float32

SLABS = 128
REPS = 4
SIDE = 8
CLUSTERS = 4
SIZE = 256
COLS = 128
GROUPS = 2
HALF = COLS // GROUPS
WIDE = CLUSTERS * HALF
QUARTER = SIZE // REPS
RANK = 32
PAIRS = 8
CHUNK = 8
SETS = SLABS // CHUNK
SELF_SET = 3
STEP = 4
STAGES = SETS // STEP


def wrap(value):
    value = jnp.where(value >= SIDE, value - SIDE, value)
    return jnp.where(value < 0, value + SIDE, value)


def ring(slab, i):
    core = lax.rem(slab, 2)
    z = lax.rem(slab // 2, SIDE)
    y = slab // (2 * SIDE)
    j = 15 - i
    a, b = 1 + j // 4, j % 4
    turns = [(a, b), (-a, -b), (-b, a), (b, -a)]
    if isinstance(i, int):
        if i == SELF_SET:
            turns = [(4, 0), (4, 4), (0, 4), (0, 0)]
    else:
        odd = i == SELF_SET
        turns[1] = (jnp.where(odd, 4, -a), jnp.where(odd, 4, -b))
        turns[3] = (jnp.where(odd, 0, b), jnp.where(odd, 0, -a))
    places = [(wrap(y + p) * SIDE + wrap(z + q)) * 2 for p, q in turns]
    return [p + 1 - core for p in places] + [p + core for p in places]


def swap_halves(x):
    return pltpu.roll(x, HALF, 1)


def kernel(
    pairs_in, owners_in, start_in, self_in, near_in, far_in, first, second,
    pairs, owners,
    start, self_row, near, near_t, far, far_t, vec, self_wide, masks,
    sbuf, rbuf, nextvec, doubled, fwd, bwd, acc, nx_part, nx_got, ns_out, ns_got, xr,
    load_sem, out_sem, a2a_s, a2a_r, x_s, x_r, vn_s, vn_r, rl_s, rl_r, nx_s, nx_r, ns_s, ns_r,
):
    slab, rep = lax.axis_index("clus"), lax.axis_index("rep")
    after = jnp.where(slab == SLABS - 1, 0, slab + 1)
    before = jnp.where(slab == 0, SLABS - 1, slab - 1)
    rep_peers = [lax.rem(rep + k, REPS) for k in (2, 1, 3)]

    loads = [
        pltpu.make_async_copy(start_in, start, load_sem.at[0]),
        pltpu.make_async_copy(far_in, far, load_sem.at[1]),
        pltpu.make_async_copy(owners_in, owners, load_sem.at[2]),
        pltpu.make_async_copy(self_in, self_row, load_sem.at[3]),
        pltpu.make_async_copy(pairs_in, pairs, load_sem.at[4]),
    ] + [
        pltpu.make_async_copy(near_in.at[n], near.at[:, pl.ds(n * SIZE, SIZE)], load_sem.at[5 + n])
        for n in range(PAIRS)
    ]
    for load in loads:
        load.start()

    greeting = pltpu.get_barrier_semaphore()

    def greet(peer):
        pl.semaphore_signal(greeting, inc=1, device_id=(peer, rep), device_id_type=MESH)

    for i in range(SETS):
        for e, peer in enumerate(ring(slab, i)):
            if (i, e) != (SELF_SET, CHUNK - 1):
                greet(peer)
    for peer in rep_peers:
        pl.semaphore_signal(greeting, inc=1, device_id=(slab, peer), device_id_type=MESH)

    lane = lax.broadcasted_iota(jnp.int32, (16, COLS), 1)
    low = (lane < HALF).astype(F32).astype(BF16)
    high = (lane >= HALF).astype(F32).astype(BF16)
    block = lax.broadcasted_iota(jnp.int32, (16, 2 * WIDE), 1) // HALF
    for c in range(2 * CLUSTERS):
        masks[c] = (block == c).astype(F32).astype(BF16)

    def merged(x, y):
        rows = x.shape[0]
        x3, y3 = x.reshape(rows // 16, 16, COLS), y.reshape(rows // 16, 16, COLS)
        return (x3 * low[None] + y3 * high[None]).reshape(rows, COLS)

    loads[0].wait()
    for pair in range(CLUSTERS // 2):
        even = start[pl.ds(2 * pair * SIZE, SIZE), :]
        odd = start[pl.ds((2 * pair + 1) * SIZE, SIZE), :]
        part = (REPS, QUARTER, COLS)
        vec[0, 0, :, :, pl.ds(pair * COLS, COLS)] = merged(even, swap_halves(odd)).reshape(part)
        vec[0, 1, :, :, pl.ds(pair * COLS, COLS)] = merged(swap_halves(even), odd).reshape(part)

    def coefficients(m, g, first=0, last=STAGES):
        values = vec[m, g].reshape(SIZE, WIDE)

        def multiply(ends):
            factors = jnp.concatenate([far[end] for end in ends], axis=0)
            return jnp.dot(factors, values, preferred_element_type=F32).astype(BF16)

        def pick(full, ends):
            for e, end in enumerate(ends):
                mask = masks[owners[end], :, pl.ds(0, WIDE)]
                halves = []
                for top in (0, 16):
                    rows = full[e * RANK + top : e * RANK + top + 16, :] * mask
                    folded = rows[:, :COLS] + rows[:, COLS:]
                    halves.append(folded + swap_halves(folded))
                sbuf[m, g, end] = halves[0] * low + halves[1] * high

        def send(stage, k, e, end):
            copy = pltpu.make_async_remote_copy(
                sbuf.at[m, g, end], rbuf.at[m, g, slab], a2a_s.at[m, g], a2a_r.at[m, g, stage],
                device_id=(end, rep), device_id_type=MESH,
            )
            if k == SELF_SET and e == CHUNK - 1:
                pl.when(stage > 0)(copy.start)
            else:
                copy.start()

        def step(stage, _):
            sets = [ring(slab, stage * STEP + k) for k in range(STEP)]
            full = [multiply(ends) for ends in sets]
            for k, ends in enumerate(sets):
                pick(full[k], ends)
            for k, ends in enumerate(sets):
                for e, end in enumerate(ends):
                    send(stage, k, e, end)
            return 0

        lax.fori_loop(first, last, step, 0)
        if first == 0:
            rbuf[m, g, slab] = sbuf[m, g, slab]

    def sent(m, g):
        others = pl.ds(0, SLABS - 1)
        return pltpu.make_async_remote_copy(
            sbuf.at[m, g, others], rbuf.at[m, g, others], a2a_s.at[m, g], a2a_r.at[m, g, 0],
            device_id=(slab, rep), device_id_type=MESH,
        )

    def received(m, g, stage, count):
        some = pl.ds(0, count)
        return pltpu.make_async_remote_copy(
            sbuf.at[m, g, some], rbuf.at[m, g, some], a2a_s.at[m, g], a2a_r.at[m, g, stage],
            device_id=(slab, rep), device_id_type=MESH,
        )

    def next_vector(m, g):
        return pltpu.make_async_remote_copy(
            vec.at[m, g, rep], nextvec.at[m, g, rep], vn_s.at[m, g], vn_r.at[m, g],
            device_id=(before, rep), device_id_type=MESH,
        )

    def relays(m, g):
        return [
            pltpu.make_async_remote_copy(
                nextvec.at[m, g, rep], nextvec.at[m, g, rep], rl_s.at[m, g, k], rl_r.at[m, g, k],
                device_id=(slab, peer), device_id_type=MESH,
            )
            for k, peer in enumerate(rep_peers)
        ]

    def next_parts(m, g):
        return [
            pltpu.make_async_remote_copy(
                nx_part.at[m, g, peer], nx_got.at[m, g, rep], nx_s.at[m, g, k], nx_r.at[m, g, k],
                device_id=(slab, peer), device_id_type=MESH,
            )
            for k, peer in enumerate(rep_peers)
        ]

    def next_sum(m, g):
        return pltpu.make_async_remote_copy(
            ns_out.at[m, g], ns_got.at[m, g], ns_s.at[m, g], ns_r.at[m, g],
            device_id=(after, rep), device_id_type=MESH,
        )

    def exchanges(m, g):
        return [
            pltpu.make_async_remote_copy(
                xr.at[m, g, rep], xr.at[m, g, rep], x_s.at[m, g, k], x_r.at[m, g, k],
                device_id=(slab, peer), device_id_type=MESH,
            )
            for k, peer in enumerate(rep_peers)
        ]

    def double(m, g, source, base):
        for pair in range(CLUSTERS // 2):
            both = source[m, g, :, :, pl.ds(pair * COLS, COLS)].reshape(SIZE, COLS)
            turned = swap_halves(both)
            doubled[g, base + 2 * pair] = merged(both, turned)
            doubled[g, base + 2 * pair + 1] = merged(turned, both)

    def backward(m, g):
        double(m, g, vec, 0)

        def place(n, _):
            a, b = pairs[0, n], pairs[1, n]
            values = doubled[g, a].reshape(SIZE // 16, 16, COLS)
            for k in range(2 * WIDE // COLS):
                mask = masks[b, :, pl.ds(k * COLS, COLS)]
                bwd[n, :, pl.ds(k * COLS, COLS)] = (values * mask[None]).reshape(SIZE, COLS)
            return 0

        lax.fori_loop(0, PAIRS, place, 0)
        terms = jnp.dot(near_t[...], bwd[...].reshape(PAIRS * SIZE, 2 * WIDE), preferred_element_type=F32)
        nx_part[m, g] = terms[:, WIDE:].astype(BF16).reshape(REPS, QUARTER, WIDE)
        acc[m, g] = terms[:, :WIDE]
        nx_got[m, g, rep] = nx_part[m, g, rep]
        for copy in next_parts(m, g):
            copy.start()

    def forward(m, g):
        for copy in relays(m, g):
            copy.wait_recv()
        double(m, g, nextvec, CLUSTERS)

        def place(n, _):
            a, b = pairs[0, n], pairs[1, n]
            values = doubled[g, b].reshape(SIZE // 16, 16, COLS)
            for k in range(WIDE // COLS):
                mask = masks[a, :, pl.ds(k * COLS, COLS)]
                fwd[n, :, pl.ds(k * COLS, COLS)] = (values * mask[None]).reshape(SIZE, COLS)
            return 0

        lax.fori_loop(0, PAIRS, place, 0)
        acc[m, g] += jnp.dot(near[...], fwd[...].reshape(PAIRS * SIZE, WIDE), preferred_element_type=F32)

    def sum_next(m, g):
        for copy in next_parts(m, g):
            copy.wait_recv()
        total = nx_got[m, g, 0].astype(F32)
        for s in range(1, REPS):
            total += nx_got[m, g, s].astype(F32)
        ns_out[m, g] = total.astype(BF16)
        next_sum(m, g).start()

    def far_terms(m, g):
        def step(stage, _):
            if isinstance(stage, int):
                received(m, g, stage, STEP * CHUNK - 1).wait_recv()
            else:
                received(m, g, stage, STEP * CHUNK).wait_recv()
            tiles = []
            for k in range(STEP):
                for end in ring(slab, stage * STEP + k):
                    mask = masks[owners[end], :, pl.ds(0, WIDE)]
                    got = rbuf[m, g, end]
                    turned = swap_halves(got)
                    for part in (got * low + turned * high, turned * low + got * high):
                        tiles.append(jnp.concatenate([part] * (WIDE // COLS), axis=1) * mask)
            spread = jnp.concatenate(tiles, axis=0)
            acc[m, g] += jnp.dot(far_t[stage], spread, preferred_element_type=F32)
            return 0

        step(0, 0)
        lax.fori_loop(1, STAGES, step, 0)
        next_sum(m, g).wait_recv()
        mine = pl.ds(pl.multiple_of(rep * QUARTER, QUARTER), QUARTER)
        acc[m, g, mine, :] += ns_got[m, g].astype(F32)
        xr[m, g, rep] = acc[m, g].astype(BF16)
        for copy in exchanges(m, g):
            copy.start()

    def image(m, g):
        for copy in exchanges(m, g):
            copy.wait_recv()
        total = self_wide[...] * vec[m, g].reshape(SIZE, WIDE).astype(F32)
        for s in range(REPS):
            total += xr[m, g, s].astype(F32)
        vec[m + 1, g] = total.astype(BF16).reshape(REPS, QUARTER, WIDE)

    def write(m, out):
        return pltpu.make_async_copy(vec.at[m + 1], out, out_sem.at[m])

    loads[1].wait()
    loads[2].wait()
    pl.semaphore_wait(greeting, SLABS - 1 + REPS - 1)
    next_vector(0, 0).start()
    next_vector(0, 1).start()
    coefficients(0, 0)

    for load in loads[3:]:
        load.wait()
    for n in range(PAIRS):
        near_t[:, pl.ds(n * SIZE, SIZE)] = near[:, pl.ds(n * SIZE, SIZE)].T
    backward(0, 0)
    backward(0, 1)

    def pass_on(m, g):
        next_vector(m, g).wait_recv()
        for copy in relays(m, g):
            copy.start()

    pass_on(0, 0)
    pass_on(0, 1)
    coefficients(0, 1)
    sum_next(0, 0)
    sum_next(0, 1)
    forward(0, 0)

    for i in range(SETS):
        tile = jnp.concatenate([far[end] for end in ring(slab, i)], axis=0)
        far_t[i // STEP, :, pl.ds((i % STEP) * CHUNK * RANK, CHUNK * RANK)] = tile.T
    wide = [
        jnp.broadcast_to(
            jnp.concatenate([self_row[2 * c : 2 * c + 1, :], self_row[2 * c + 1 : 2 * c + 2, :]], axis=1),
            (HALF, SIZE),
        )
        for c in range(CLUSTERS)
    ]
    self_wide[...] = jnp.concatenate(wide, axis=0).T

    far_terms(0, 0)
    image(0, 0)
    next_vector(1, 0).start()
    coefficients(1, 0)
    forward(0, 1)
    far_terms(0, 1)
    backward(1, 0)
    pass_on(1, 0)
    sum_next(1, 0)
    image(0, 1)
    next_vector(1, 1).start()
    coefficients(1, 1)
    forward(1, 0)
    backward(1, 1)
    far_terms(1, 0)
    pass_on(1, 1)
    sum_next(1, 1)
    write(0, first).start()
    forward(1, 1)
    image(1, 0)
    far_terms(1, 1)
    image(1, 1)
    write(1, second).start()

    for m in range(2):
        for g in range(GROUPS):
            sent(m, g).wait_send()
            next_vector(m, g).wait_send()
            next_sum(m, g).wait_send()
            for copy in relays(m, g) + next_parts(m, g) + exchanges(m, g):
                copy.wait_send()
    write(0, first).wait()
    write(1, second).wait()


def lay_out(first, second, first_out, second_out):
    lane = lax.broadcasted_iota(jnp.int32, (SIZE, COLS), 1)
    for source, out in ((first, first_out), (second, second_out)):
        for pair in range(CLUSTERS // 2):
            lanes = pl.ds(pair * COLS, COLS)
            a = source[0, :, :, lanes].reshape(SIZE, COLS)
            b = source[1, :, :, lanes].reshape(SIZE, COLS)
            out[pl.ds(2 * pair * SIZE, SIZE), :] = jnp.where(lane < HALF, a, swap_halves(b))
            out[pl.ds((2 * pair + 1) * SIZE, SIZE), :] = jnp.where(lane < HALF, swap_halves(a), b)


def local(start_vector, self_term, near_blocks, near_pairs, far_factor, far_cluster):
    panels, columns = start_vector.shape
    factors = far_factor.reshape(far_factor.shape[2:])
    owners = far_cluster.reshape(-1)
    pairs = near_pairs.T
    self_rows = self_term.reshape(panels // COLS, COLS)
    vmem, dma = pltpu.VMEM, pltpu.SemaphoreType.DMA
    image = jax.ShapeDtypeStruct((panels, columns), BF16)
    grouped = jax.ShapeDtypeStruct((GROUPS, REPS, QUARTER, WIDE), BF16)
    both = (2, GROUPS)
    scratch = [
        pltpu.SMEM(pairs.shape, jnp.int32),
        pltpu.SMEM(owners.shape, jnp.int32),
        vmem((panels, columns), BF16),
        vmem(self_rows.shape, F32),
        vmem((SIZE, PAIRS * SIZE), BF16),
        vmem((SIZE, PAIRS * SIZE), BF16),
        vmem(factors.shape, BF16),
        vmem((STAGES, SIZE, STEP * CHUNK * RANK), BF16),
        vmem((3, GROUPS, REPS, QUARTER, WIDE), BF16),
        vmem((SIZE, WIDE), F32),
        vmem((2 * CLUSTERS, 16, 2 * WIDE), BF16),
        vmem(both + (SLABS, 16, COLS), BF16),
        vmem(both + (SLABS, 16, COLS), BF16),
        vmem(both + (REPS, QUARTER, WIDE), BF16),
        vmem((GROUPS, 2 * CLUSTERS, SIZE, COLS), BF16),
        vmem((PAIRS, SIZE, WIDE), BF16),
        vmem((PAIRS, SIZE, 2 * WIDE), BF16),
        vmem(both + (SIZE, WIDE), F32),
        vmem(both + (REPS, QUARTER, WIDE), BF16),
        vmem(both + (REPS, QUARTER, WIDE), BF16),
        vmem(both + (QUARTER, WIDE), BF16),
        vmem(both + (QUARTER, WIDE), BF16),
        vmem(both + (REPS, SIZE, WIDE), BF16),
        dma((5 + PAIRS,)),
        dma((2,)),
        dma(both), dma(both + (STAGES,)),
        dma(both + (3,)), dma(both + (3,)),
        dma(both), dma(both),
        dma(both + (3,)), dma(both + (3,)),
        dma(both + (3,)), dma(both + (3,)),
        dma(both), dma(both),
    ]
    hbm = pl.BlockSpec(memory_space=pl.ANY)
    whole = pl.BlockSpec(memory_space=pltpu.VMEM)
    images = pl.pallas_call(
        kernel,
        out_shape=(grouped, grouped),
        in_specs=[hbm] * 6,
        out_specs=(hbm, hbm),
        scratch_shapes=scratch,
        compiler_params=pltpu.CompilerParams(
            collective_id=0, has_side_effects=True, vmem_limit_bytes=60 * 1024 * 1024
        ),
        name="two_products",
    )(pairs, owners, start_vector, self_rows, near_blocks, factors)
    return pl.pallas_call(
        lay_out,
        out_shape=(image, image),
        in_specs=[whole, whole],
        out_specs=(whole, whole),
        name="lay_out",
    )(*images)


def solution(mesh):
    placed = (
        P("clus", None),
        P("clus"),
        P(("clus", "rep"), None, None),
        P(("clus", "rep"), None),
        P("clus", "rep", None, None, None),
        P("clus", "rep", None),
    )
    return jax.shard_map(
        local,
        mesh=mesh,
        in_specs=placed,
        out_specs=(P("clus", None), P("clus", None)),
        check_vma=False,
    )
```

```python
import functools

import jax
import jax.numpy as jnp
from jax import lax
from jax.experimental import pallas as pl
from jax.experimental.pallas import tpu as pltpu
from jax.sharding import PartitionSpec as P

MESH = pl.DeviceIdType.MESH
BF16 = jnp.bfloat16
F32 = jnp.float32

SLABS = 128
REPS = 4
SIDE = 8
CLUSTERS = 4
SIZE = 256
COLS = 128
GROUPS = 2
HALF = COLS // GROUPS
WIDE = CLUSTERS * HALF
QUARTER = SIZE // REPS
RANK = 32
PAIRS = 8
CHUNK = 8
SETS = SLABS // CHUNK
SELF_SET = 3
STEP = 4
STAGES = SETS // STEP


def wrap(value):
    value = jnp.where(value >= SIDE, value - SIDE, value)
    return jnp.where(value < 0, value + SIDE, value)


def ring(slab, i):
    core = lax.rem(slab, 2)
    z = lax.rem(slab // 2, SIDE)
    y = slab // (2 * SIDE)
    j = 15 - i
    a, b = 1 + j // 4, j % 4
    turns = [(a, b), (-a, -b), (-b, a), (b, -a)]
    if isinstance(i, int):
        if i == SELF_SET:
            turns = [(4, 0), (4, 4), (0, 4), (0, 0)]
    else:
        odd = i == SELF_SET
        turns[1] = (jnp.where(odd, 4, -a), jnp.where(odd, 4, -b))
        turns[3] = (jnp.where(odd, 0, b), jnp.where(odd, 0, -a))
    places = [(wrap(y + p) * SIDE + wrap(z + q)) * 2 for p, q in turns]
    return [p + 1 - core for p in places] + [p + core for p in places]


def swap_halves(x):
    return pltpu.roll(x, HALF, 1)


def kernel(
    pairs_in, owners_in, start_in, self_in, near_in, far_in, first, second,
    pairs, owners,
    start, self_row, near, near_t, far, far_t, vec, self_wide, masks,
    sbuf, rbuf, nextvec, doubled, fwd, bwd, acc, nx_part, nx_got, ns_out, ns_got, xp, xr,
    load_sem, out_sem, a2a_s, a2a_r, x_s, x_r, g_s, g_r, vn_s, vn_r, rl_s, rl_r, nx_s, nx_r, ns_s, ns_r,
):
    slab, rep = lax.axis_index("clus"), lax.axis_index("rep")
    after = jnp.where(slab == SLABS - 1, 0, slab + 1)
    before = jnp.where(slab == 0, SLABS - 1, slab - 1)
    rep_peers = [lax.rem(rep + k, REPS) for k in (2, 1, 3)]

    loads = [
        pltpu.make_async_copy(start_in, start, load_sem.at[0]),
        pltpu.make_async_copy(far_in, far, load_sem.at[1]),
        pltpu.make_async_copy(owners_in, owners, load_sem.at[2]),
        pltpu.make_async_copy(self_in, self_row, load_sem.at[3]),
        pltpu.make_async_copy(pairs_in, pairs, load_sem.at[4]),
    ] + [
        pltpu.make_async_copy(near_in.at[n], near.at[:, pl.ds(n * SIZE, SIZE)], load_sem.at[5 + n])
        for n in range(PAIRS)
    ]
    for load in loads[:3]:
        load.start()

    greeting = pltpu.get_barrier_semaphore()

    def greet(peer):
        pl.semaphore_signal(greeting, inc=1, device_id=(peer, rep), device_id_type=MESH)

    for i in range(SETS):
        for e, peer in enumerate(ring(slab, i)):
            if (i, e) != (SELF_SET, CHUNK - 1):
                greet(peer)
    for peer in rep_peers:
        pl.semaphore_signal(greeting, inc=1, device_id=(slab, peer), device_id_type=MESH)

    for load in loads[3:]:
        load.start()

    lane = lax.broadcasted_iota(jnp.int32, (16, COLS), 1)
    low = (lane < HALF).astype(F32).astype(BF16)
    high = (lane >= HALF).astype(F32).astype(BF16)
    block = lax.broadcasted_iota(jnp.int32, (16, 2 * WIDE), 1) // HALF
    for c in range(2 * CLUSTERS):
        masks[c] = (block == c).astype(F32).astype(BF16)

    def merged(x, y):
        rows = x.shape[0]
        x3, y3 = x.reshape(rows // 16, 16, COLS), y.reshape(rows // 16, 16, COLS)
        return (x3 * low[None] + y3 * high[None]).reshape(rows, COLS)

    loads[0].wait()
    for pair in range(CLUSTERS // 2):
        even = start[pl.ds(2 * pair * SIZE, SIZE), :]
        odd = start[pl.ds((2 * pair + 1) * SIZE, SIZE), :]
        part = (REPS, QUARTER, COLS)
        vec[0, 0, :, :, pl.ds(pair * COLS, COLS)] = merged(even, swap_halves(odd)).reshape(part)
        vec[0, 1, :, :, pl.ds(pair * COLS, COLS)] = merged(swap_halves(even), odd).reshape(part)

    def coefficients(m, g):
        values = vec[m, g].reshape(SIZE, WIDE)

        def multiply(ends):
            factors = jnp.concatenate([far[end] for end in ends], axis=0)
            return jnp.dot(factors, values, preferred_element_type=F32).astype(BF16)

        def pick(full, ends):
            for e, end in enumerate(ends):
                mask = masks[owners[end], :, pl.ds(0, WIDE)]
                halves = []
                for top in (0, 16):
                    rows = full[e * RANK + top : e * RANK + top + 16, :] * mask
                    folded = rows[:, :COLS] + rows[:, COLS:]
                    halves.append(folded + swap_halves(folded))
                sbuf[m, g, end] = halves[0] * low + halves[1] * high

        def send(stage, k, e, end):
            copy = pltpu.make_async_remote_copy(
                sbuf.at[m, g, end], rbuf.at[m, g, slab], a2a_s.at[m, g], a2a_r.at[m, g, stage],
                device_id=(end, rep), device_id_type=MESH,
            )
            if k == SELF_SET and e == CHUNK - 1:
                pl.when(stage > 0)(copy.start)
            else:
                copy.start()

        def step(stage, _):
            sets = [ring(slab, stage * STEP + k) for k in range(STEP)]
            full = [multiply(ends) for ends in sets]
            for k, ends in enumerate(sets):
                pick(full[k], ends)
            for k, ends in enumerate(sets):
                for e, end in enumerate(ends):
                    send(stage, k, e, end)
            return 0

        lax.fori_loop(0, STAGES, step, 0)
        rbuf[m, g, slab] = sbuf[m, g, slab]

    def sent(m, g):
        others = pl.ds(0, SLABS - 1)
        return pltpu.make_async_remote_copy(
            sbuf.at[m, g, others], rbuf.at[m, g, others], a2a_s.at[m, g], a2a_r.at[m, g, 0],
            device_id=(slab, rep), device_id_type=MESH,
        )

    def received(m, g, stage, count):
        some = pl.ds(0, count)
        return pltpu.make_async_remote_copy(
            sbuf.at[m, g, some], rbuf.at[m, g, some], a2a_s.at[m, g], a2a_r.at[m, g, stage],
            device_id=(slab, rep), device_id_type=MESH,
        )

    def next_vector(m, g):
        return pltpu.make_async_remote_copy(
            vec.at[m, g, rep], nextvec.at[m, g, rep], vn_s.at[m, g], vn_r.at[m, g],
            device_id=(before, rep), device_id_type=MESH,
        )

    def relays(m, g):
        return [
            pltpu.make_async_remote_copy(
                nextvec.at[m, g, rep], nextvec.at[m, g, rep], rl_s.at[m, g, k], rl_r.at[m, g, k],
                device_id=(slab, peer), device_id_type=MESH,
            )
            for k, peer in enumerate(rep_peers)
        ]

    def next_parts(m, g):
        return [
            pltpu.make_async_remote_copy(
                nx_part.at[m, g, peer], nx_got.at[m, g, rep], nx_s.at[m, g, k], nx_r.at[m, g, k],
                device_id=(slab, peer), device_id_type=MESH,
            )
            for k, peer in enumerate(rep_peers)
        ]

    def next_sum(m, g):
        return pltpu.make_async_remote_copy(
            ns_out.at[m, g], ns_got.at[m, g], ns_s.at[m, g], ns_r.at[m, g],
            device_id=(after, rep), device_id_type=MESH,
        )

    def exchanges(m, g):
        return [
            pltpu.make_async_remote_copy(
                xp.at[m, g, peer], xr.at[m, g, rep], x_s.at[m, g, k], x_r.at[m, g, k],
                device_id=(slab, peer), device_id_type=MESH,
            )
            for k, peer in enumerate(rep_peers)
        ]

    def gathers(m, g):
        return [
            pltpu.make_async_remote_copy(
                vec.at[m + 1, g, rep], vec.at[m + 1, g, rep], g_s.at[m, g, k], g_r.at[m, g, k],
                device_id=(slab, peer), device_id_type=MESH,
            )
            for k, peer in enumerate(rep_peers)
        ]

    def double(m, g, source, base):
        for pair in range(CLUSTERS // 2):
            both = source[m, g, :, :, pl.ds(pair * COLS, COLS)].reshape(SIZE, COLS)
            turned = swap_halves(both)
            doubled[g, base + 2 * pair] = merged(both, turned)
            doubled[g, base + 2 * pair + 1] = merged(turned, both)

    def backward(m, g):
        double(m, g, vec, 0)

        def place(n, _):
            a, b = pairs[0, n], pairs[1, n]
            values = doubled[g, a].reshape(SIZE // 16, 16, COLS)
            for k in range(2 * WIDE // COLS):
                mask = masks[b, :, pl.ds(k * COLS, COLS)]
                bwd[n, :, pl.ds(k * COLS, COLS)] = (values * mask[None]).reshape(SIZE, COLS)
            return 0

        lax.fori_loop(0, PAIRS, place, 0)
        terms = jnp.dot(near_t[...], bwd[...].reshape(PAIRS * SIZE, 2 * WIDE), preferred_element_type=F32)
        nx_part[m, g] = terms[:, WIDE:].astype(BF16).reshape(REPS, QUARTER, WIDE)
        acc[m, g] = terms[:, :WIDE]
        nx_got[m, g, rep] = nx_part[m, g, rep]
        for copy in next_parts(m, g):
            copy.start()

    def forward(m, g):
        for copy in relays(m, g):
            copy.wait_recv()
        double(m, g, nextvec, CLUSTERS)

        def place(n, _):
            a, b = pairs[0, n], pairs[1, n]
            values = doubled[g, b].reshape(SIZE // 16, 16, COLS)
            for k in range(WIDE // COLS):
                mask = masks[a, :, pl.ds(k * COLS, COLS)]
                fwd[n, :, pl.ds(k * COLS, COLS)] = (values * mask[None]).reshape(SIZE, COLS)
            return 0

        lax.fori_loop(0, PAIRS, place, 0)
        acc[m, g] += jnp.dot(near[...], fwd[...].reshape(PAIRS * SIZE, WIDE), preferred_element_type=F32)

    def sum_next(m, g):
        for copy in next_parts(m, g):
            copy.wait_recv()
        total = nx_got[m, g, 0].astype(F32)
        for s in range(1, REPS):
            total += nx_got[m, g, s].astype(F32)
        ns_out[m, g] = total.astype(BF16)
        next_sum(m, g).start()

    def far_terms(m, g):
        def step(stage, _):
            if isinstance(stage, int):
                received(m, g, stage, STEP * CHUNK - 1).wait_recv()
            else:
                received(m, g, stage, STEP * CHUNK).wait_recv()
            tiles = []
            for k in range(STEP):
                for end in ring(slab, stage * STEP + k):
                    mask = masks[owners[end], :, pl.ds(0, WIDE)]
                    got = rbuf[m, g, end]
                    turned = swap_halves(got)
                    for part in (got * low + turned * high, turned * low + got * high):
                        tiles.append(jnp.concatenate([part] * (WIDE // COLS), axis=1) * mask)
            spread = jnp.concatenate(tiles, axis=0)
            acc[m, g] += jnp.dot(far_t[stage], spread, preferred_element_type=F32)
            return 0

        step(0, 0)
        lax.fori_loop(1, STAGES, step, 0)

    def exchange(m, g):
        next_sum(m, g).wait_recv()
        mine = pl.ds(pl.multiple_of(rep * QUARTER, QUARTER), QUARTER)
        acc[m, g, mine, :] += ns_got[m, g].astype(F32)
        xp[m, g] = acc[m, g].astype(BF16).reshape(REPS, QUARTER, WIDE)
        xr[m, g, rep] = xp[m, g, rep]
        for copy in exchanges(m, g):
            copy.start()

    def reduce(m, g):
        for copy in exchanges(m, g):
            copy.wait_recv()
        mine = pl.ds(pl.multiple_of(rep * QUARTER, QUARTER), QUARTER)
        total = self_wide[mine, :] * vec[m, g, rep].astype(F32)
        for s in range(REPS):
            total += xr[m, g, s].astype(F32)
        vec[m + 1, g, rep] = total.astype(BF16)
        for copy in gathers(m, g):
            copy.start()
        if m == 0:
            next_vector(1, g).start()

    def image(m, g):
        for copy in gathers(m, g):
            copy.wait_recv()

    def write(m, out):
        return pltpu.make_async_copy(vec.at[m + 1], out, out_sem.at[m])

    loads[1].wait()
    loads[2].wait()
    pl.semaphore_wait(greeting, SLABS - 1 + REPS - 1)
    next_vector(0, 0).start()
    next_vector(0, 1).start()
    coefficients(0, 0)

    for load in loads[3:]:
        load.wait()
    for n in range(PAIRS):
        near_t[:, pl.ds(n * SIZE, SIZE)] = near[:, pl.ds(n * SIZE, SIZE)].T
    backward(0, 0)
    backward(0, 1)

    def pass_on(m, g):
        next_vector(m, g).wait_recv()
        for copy in relays(m, g):
            copy.start()

    pass_on(0, 0)
    pass_on(0, 1)
    coefficients(0, 1)
    sum_next(0, 0)
    sum_next(0, 1)
    forward(0, 0)

    for i in range(SETS):
        tile = jnp.concatenate([far[end] for end in ring(slab, i)], axis=0)
        far_t[i // STEP, :, pl.ds((i % STEP) * CHUNK * RANK, CHUNK * RANK)] = tile.T
    wide = [
        jnp.broadcast_to(
            jnp.concatenate([self_row[2 * c : 2 * c + 1, :], self_row[2 * c + 1 : 2 * c + 2, :]], axis=1),
            (HALF, SIZE),
        )
        for c in range(CLUSTERS)
    ]
    self_wide[...] = jnp.concatenate(wide, axis=0).T

    far_terms(0, 0)
    exchange(0, 0)
    forward(0, 1)
    reduce(0, 0)
    image(0, 0)
    coefficients(1, 0)
    far_terms(0, 1)
    exchange(0, 1)
    backward(1, 0)
    pass_on(1, 0)
    reduce(0, 1)
    sum_next(1, 0)
    image(0, 1)
    coefficients(1, 1)
    forward(1, 0)
    backward(1, 1)
    far_terms(1, 0)
    exchange(1, 0)
    pass_on(1, 1)
    sum_next(1, 1)
    reduce(1, 0)
    write(0, first).start()
    forward(1, 1)
    far_terms(1, 1)
    exchange(1, 1)
    image(1, 0)
    reduce(1, 1)
    image(1, 1)
    write(1, second).start()

    for m in range(2):
        for g in range(GROUPS):
            sent(m, g).wait_send()
            next_vector(m, g).wait_send()
            next_sum(m, g).wait_send()
            for copy in relays(m, g) + next_parts(m, g) + exchanges(m, g) + gathers(m, g):
                copy.wait_send()
    write(0, first).wait()
    write(1, second).wait()


def lay_out(first, second, first_out, second_out):
    lane = lax.broadcasted_iota(jnp.int32, (SIZE, COLS), 1)
    for source, out in ((first, first_out), (second, second_out)):
        for pair in range(CLUSTERS // 2):
            lanes = pl.ds(pair * COLS, COLS)
            a = source[0, :, :, lanes].reshape(SIZE, COLS)
            b = source[1, :, :, lanes].reshape(SIZE, COLS)
            out[pl.ds(2 * pair * SIZE, SIZE), :] = jnp.where(lane < HALF, a, swap_halves(b))
            out[pl.ds((2 * pair + 1) * SIZE, SIZE), :] = jnp.where(lane < HALF, swap_halves(a), b)


def local(start_vector, self_term, near_blocks, near_pairs, far_factor, far_cluster):
    panels, columns = start_vector.shape
    factors = far_factor.reshape(far_factor.shape[2:])
    owners = far_cluster.reshape(-1)
    pairs = near_pairs.T
    self_rows = self_term.reshape(panels // COLS, COLS)
    vmem, dma = pltpu.VMEM, pltpu.SemaphoreType.DMA
    image = jax.ShapeDtypeStruct((panels, columns), BF16)
    grouped = jax.ShapeDtypeStruct((GROUPS, REPS, QUARTER, WIDE), BF16)
    both = (2, GROUPS)
    scratch = [
        pltpu.SMEM(pairs.shape, jnp.int32),
        pltpu.SMEM(owners.shape, jnp.int32),
        vmem((panels, columns), BF16),
        vmem(self_rows.shape, F32),
        vmem((SIZE, PAIRS * SIZE), BF16),
        vmem((SIZE, PAIRS * SIZE), BF16),
        vmem(factors.shape, BF16),
        vmem((STAGES, SIZE, STEP * CHUNK * RANK), BF16),
        vmem((3, GROUPS, REPS, QUARTER, WIDE), BF16),
        vmem((SIZE, WIDE), F32),
        vmem((2 * CLUSTERS, 16, 2 * WIDE), BF16),
        vmem(both + (SLABS, 16, COLS), BF16),
        vmem(both + (SLABS, 16, COLS), BF16),
        vmem(both + (REPS, QUARTER, WIDE), BF16),
        vmem((GROUPS, 2 * CLUSTERS, SIZE, COLS), BF16),
        vmem((PAIRS, SIZE, WIDE), BF16),
        vmem((PAIRS, SIZE, 2 * WIDE), BF16),
        vmem(both + (SIZE, WIDE), F32),
        vmem(both + (REPS, QUARTER, WIDE), BF16),
        vmem(both + (REPS, QUARTER, WIDE), BF16),
        vmem(both + (QUARTER, WIDE), BF16),
        vmem(both + (QUARTER, WIDE), BF16),
        vmem(both + (REPS, QUARTER, WIDE), BF16),
        vmem(both + (REPS, QUARTER, WIDE), BF16),
        dma((5 + PAIRS,)),
        dma((2,)),
        dma(both), dma(both + (STAGES,)),
        dma(both + (3,)), dma(both + (3,)),
        dma(both + (3,)), dma(both + (3,)),
        dma(both), dma(both),
        dma(both + (3,)), dma(both + (3,)),
        dma(both + (3,)), dma(both + (3,)),
        dma(both), dma(both),
    ]
    hbm = pl.BlockSpec(memory_space=pl.ANY)
    whole = pl.BlockSpec(memory_space=pltpu.VMEM)
    images = pl.pallas_call(
        kernel,
        out_shape=(grouped, grouped),
        in_specs=[hbm] * 6,
        out_specs=(hbm, hbm),
        scratch_shapes=scratch,
        compiler_params=pltpu.CompilerParams(
            collective_id=0, has_side_effects=True, vmem_limit_bytes=60 * 1024 * 1024
        ),
        name="two_products",
    )(pairs, owners, start_vector, self_rows, near_blocks, factors)
    return pl.pallas_call(
        lay_out,
        out_shape=(image, image),
        in_specs=[whole, whole],
        out_specs=(whole, whole),
        name="lay_out",
    )(*images)


def solution(mesh):
    placed = (
        P("clus", None),
        P("clus"),
        P(("clus", "rep"), None, None),
        P(("clus", "rep"), None),
        P("clus", "rep", None, None, None),
        P("clus", "rep", None),
    )
    return jax.shard_map(
        local,
        mesh=mesh,
        in_specs=placed,
        out_specs=(P("clus", None), P("clus", None)),
        check_vma=False,
    )
```
